32 devices in a mesh: grp: 2 (over y), row: 4 (over x, core), col: 4 (over z).
Axes of the slice: x: 2, y: 2, z: 4, core: 2. Of those that a mesh axis runs over, the one named last changes fastest.
Arguments:
- homolog_representation: bfloat16 [192, 320, 256], P(('grp', 'row'), 'col'), parts along dimension 0, may hold values from -6 to 6
- occupancy_indicator: int32 [192, 320], P(('grp', 'row'), 'col'), parts along dimension 0, may hold values from 0 to 1, as said below
- standardize_scaling: float32 [256], replicated, may hold values from 0.5 to 1.5
- standardize_shift: float32 [256], replicated, may hold values from -3 to 3
- left_projection_matrix: bfloat16 [256, 32], replicated, may hold values from -0.375 to 0.375
- left_projection_shift: float32 [32], replicated, may hold values from -4 to 4
- right_projection_matrix: bfloat16 [256, 32], replicated, may hold values from -0.375 to 0.375
- right_projection_shift: float32 [32], replicated, may hold values from -4 to 4
- final_projection_matrix: bfloat16 [1024, 128], replicated, may hold values from -0.1875 to 0.1875
- final_projection_shift: float32 [128], replicated, may hold values from -3 to 3
Outputs:
- pair_update: bfloat16 [640, 320, 128], P(('grp', 'row'), 'col'), parts along dimension 0
The draws below stay inside these ranges and needn't reach their ends.
There are 2 independent parts, one for each index of `grp`. The reference program is written for one: setup_inputs(seed, part) draws one part's arguments, and reference() takes and returns one part's arrays. A program takes and returns all parts, laid end to end along the dimension named above; an argument that names none is the same for every part. Nothing has to cross between parts.
Inputs may be any that keep to these rules, and one draw needn't show every extreme that they name: `occupancy_indicator`: the last few sequences may be padding, all zeros. Most entries of the other sequences are 1; each residue has its own share of sequences present, from all of them down to about one per thousand; some residues are present in every sequence that is not padding.
All inputs are finite; a program needn't handle non-finite values.
Results may differ from the reference program's by a relative error of at most 0.0053.
Values may be sent and summed in bfloat16 or wider, within the bound.
A program may use at most 64 MiB of HBM per device.

```python
import jax
import jax.numpy as jnp
from jax import lax

FEATURE_WIDTH = 256
PROJ = 32
PAIR = 128
HOMOLOG_NUMBER = 96
POSITION_NUMBER = 320


def draw_occupancy_indicator(key, part):
    key = jax.random.fold_in(key, 7)
    first, second, third, fourth = jax.random.split(key, 4)
    kind = jax.random.permutation(first, POSITION_NUMBER).astype(jnp.int32) % 16
    partial_level = jax.random.randint(second, (POSITION_NUMBER,), 512, 1024)
    thresh = jnp.where(kind < 8, 1024, partial_level)
    thresh = jnp.where(kind == 14, 1, thresh)
    thresh = jnp.where(kind == 15, 64, thresh)
    roll = jax.random.randint(third, (HOMOLOG_NUMBER, POSITION_NUMBER), 0, 1024)
    present = (roll < thresh[None, :]).astype(jnp.int32)
    padded = jax.random.randint(fourth, (), 0, HOMOLOG_NUMBER // 8 + 1)
    seq_index = jnp.arange(HOMOLOG_NUMBER, dtype=jnp.int32)
    live = (seq_index < HOMOLOG_NUMBER - padded).astype(jnp.int32)
    return present * live[:, None]


def shard_levels(stream_key, shape, pieces, low, largest):
    level, own = 1.0, jax.random.fold_in(stream_key, 6)
    for position, parts in pieces:
        steps = jnp.exp(jax.random.uniform(jax.random.fold_in(own, position), (parts,), jnp.float32, low / len(pieces), largest / len(pieces)))
        level = level * jnp.repeat(steps, shape[position] // parts).reshape([-1 if axis == position else 1 for axis in range(len(shape))])
    return level


def gaussian(stream_key, extent, scale, reach, cuts=(), kind=jnp.bfloat16):
    values = scale * jax.random.normal(stream_key, extent, jnp.float32)
    if cuts:
        values = values * shard_levels(stream_key, extent, cuts, -0.22, 0.18)
    return jnp.clip(values, -reach, reach).astype(kind)


def setup_inputs(seed: int = 0, part: int = 0) -> dict:
    key_list = jax.random.split(jax.random.key(seed), 11)
    own_keys = jax.random.split(jax.random.fold_in(key_list[10], part), 11)
    homolog_representation = gaussian(own_keys[0], (HOMOLOG_NUMBER, POSITION_NUMBER, FEATURE_WIDTH), 1.0, 6.0, ((0, 4), (1, 4)))
    occupancy_indicator = draw_occupancy_indicator(jax.random.fold_in(jax.random.fold_in(key_list[10], part), 71), part)
    standardize_scaling = jnp.clip(1.0 + 0.1 * jax.random.normal(key_list[2], (FEATURE_WIDTH,), jnp.float32), 0.5, 1.5)
    standardize_shift = gaussian(key_list[3], (FEATURE_WIDTH,), 0.5, 3.0, (), jnp.float32)
    left_projection_matrix = gaussian(key_list[4], (FEATURE_WIDTH, PROJ), FEATURE_WIDTH ** -0.5, 0.375)
    left_projection_shift = gaussian(key_list[5], (PROJ,), 1.0, 4.0, (), jnp.float32)
    right_projection_matrix = gaussian(key_list[6], (FEATURE_WIDTH, PROJ), FEATURE_WIDTH ** -0.5, 0.375)
    right_projection_shift = gaussian(key_list[7], (PROJ,), 1.0, 4.0, (), jnp.float32)
    final_projection_matrix = gaussian(key_list[8], (PROJ * PROJ, PAIR), (PROJ * PROJ) ** -0.5, 0.1875)
    final_projection_shift = gaussian(key_list[9], (PAIR,), 0.5, 3.0, (), jnp.float32)
    return dict(homolog_representation=homolog_representation, occupancy_indicator=occupancy_indicator, standardize_scaling=standardize_scaling, standardize_shift=standardize_shift, left_projection_matrix=left_projection_matrix, left_projection_shift=left_projection_shift, right_projection_matrix=right_projection_matrix, right_projection_shift=right_projection_shift, final_projection_matrix=final_projection_matrix, final_projection_shift=final_projection_shift)


def reference(homolog_representation, occupancy_indicator, standardize_scaling, standardize_shift, left_projection_matrix, left_projection_shift, right_projection_matrix, right_projection_shift, final_projection_matrix, final_projection_shift):
    homolog_extent, position_extent, feature_extent = homolog_representation.shape
    width = left_projection_matrix.shape[1]
    element_number = homolog_representation.astype(jnp.float32)
    center = element_number - lax.optimization_barrier(jnp.mean(element_number, axis=-1, keepdims=True))
    spread = lax.optimization_barrier(jnp.mean(center * center, axis=-1, keepdims=True))
    normed = (center * lax.rsqrt(spread + 1e-05) * standardize_scaling + standardize_shift).astype(jnp.bfloat16)
    flat = normed.reshape(homolog_extent * position_extent, feature_extent)
    keep_flags = occupancy_indicator.astype(jnp.float32).reshape(homolog_extent * position_extent, 1)
    left = ((jnp.dot(flat, left_projection_matrix, preferred_element_type=jnp.float32) + left_projection_shift) * keep_flags).astype(jnp.bfloat16)
    right = ((jnp.dot(flat, right_projection_matrix, preferred_element_type=jnp.float32) + right_projection_shift) * keep_flags).astype(jnp.bfloat16)
    left = left.reshape(homolog_extent, position_extent, width)
    right = right.reshape(homolog_extent, position_extent, width).astype(jnp.float32)
    mask_float = occupancy_indicator.astype(jnp.float32)
    nblk = position_extent // 8
    left_blocks = jnp.transpose(left.reshape(homolog_extent, nblk, 8, width), (1, 0, 2, 3))
    mask_blocks = jnp.transpose(mask_float.reshape(homolog_extent, nblk, 8), (1, 0, 2))
    w_grid = final_projection_matrix.astype(jnp.float32).reshape(width, width, -1)

    def tile(pair):
        lblk, mblk = pair
        outer = jnp.einsum('sip,sjq->ipjq', lblk.astype(jnp.float32), right).astype(jnp.bfloat16)
        proj = jnp.einsum('ipjq,pqo->ijo', outer.astype(jnp.float32), w_grid) + final_projection_shift
        count = jnp.einsum('si,sj->ij', mblk, mask_float)
        return (proj / jnp.maximum(count, 1.0)[..., None]).astype(jnp.bfloat16)
    tiles = lax.map(tile, (left_blocks, mask_blocks))
    return tiles.reshape(position_extent, position_extent, -1)
```

```python
import functools

import jax
import jax.numpy as jnp
from jax import lax
from jax.experimental import pallas as pl
from jax.experimental.pallas import tpu as pltpu
from jax.sharding import PartitionSpec as P

MESH = pl.DeviceIdType.MESH
LANES = 128
VMEM_LIMIT = 56 * 1024 * 1024


def exchange_kernel(
    n,
    x_ref,
    gain_ref,
    bias_ref,
    wl_ref,
    bl_ref,
    wr_ref,
    br_ref,
    flat_sj_ref,
    flat_is_ref,
    mask_ref,
    lg_ref,
    rg_ref,
    ml_ref,
    mr_ref,
    norm_sj,
    norm_is,
    left_own,
    l_send,
    l_recv,
    r_send,
    r_recv,
    ml_send,
    ml_recv,
    mr_send,
    mr_recv,
):
    seqs, res, feat = x_ref.shape
    halves = feat // LANES
    tokens = seqs * res
    grp = lax.axis_index("grp")
    row = lax.axis_index("row")
    col = lax.axis_index("col")
    own = row == col

    barrier = pltpu.get_barrier_semaphore()
    for d in range(1, n):
        pl.semaphore_signal(barrier, inc=1, device_id=(grp, lax.rem(row + d, n), col), device_id_type=MESH)
        pl.semaphore_signal(barrier, inc=1, device_id=(grp, lax.rem(row + d, n), row), device_id_type=MESH)

    @pl.when(jnp.logical_not(own))
    def _():
        pl.semaphore_signal(barrier, inc=1, device_id=(grp, row, row), device_id_type=MESH)

    gain = gain_ref[...]
    bias = bias_ref[...]

    def normalize(s, carry):
        e = x_ref[s].astype(jnp.float32)
        center = e - jnp.mean(e, axis=-1, keepdims=True)
        spread = jnp.mean(center * center, axis=-1, keepdims=True)
        v = center * lax.rsqrt(spread + 1e-05) * gain + bias
        at = pl.multiple_of(s * res, 8)
        for h in range(halves):
            norm_sj[h, pl.ds(at, res), :] = v[:, h * LANES : (h + 1) * LANES]
        return carry

    lax.fori_loop(0, seqs, normalize, 0)

    def reorder(i, carry):
        at = pl.multiple_of(i * seqs, 8)
        for h in range(halves):
            norm_is[h, pl.ds(at, seqs), :] = norm_sj[h, pl.ds(i, seqs, stride=res), :]
        return carry

    lax.fori_loop(0, res, reorder, 0, unroll=4)

    def project(src, w_ref, b_ref, flat_ref):
        total = b_ref[...]
        acc = None
        for h in range(halves):
            part = lax.dot_general(
                w_ref[:, h * LANES : (h + 1) * LANES],
                src[h].astype(jnp.bfloat16),
                (((1,), (1,)), ((), ())),
                preferred_element_type=jnp.float32,
            )
            acc = part if acc is None else acc + part
        return ((acc + total) * flat_ref[...]).astype(jnp.bfloat16)

    left_own[...] = project(norm_is, wl_ref, bl_ref, flat_is_ref)

    others = (n - 1) + n - own.astype(jnp.int32)
    pl.semaphore_wait(barrier, others)

    def left_copies(d):
        target = (grp, col, lax.rem(col + d, n))
        return (
            pltpu.make_async_remote_copy(
                src_ref=left_own, dst_ref=lg_ref.at[row], send_sem=l_send.at[d], recv_sem=l_recv.at[row],
                device_id=target, device_id_type=MESH,
            ),
            pltpu.make_async_remote_copy(
                src_ref=mask_ref, dst_ref=ml_ref.at[row], send_sem=ml_send.at[d], recv_sem=ml_recv.at[row],
                device_id=target, device_id_type=MESH,
            ),
        )

    def right_copies(d):
        target = (grp, lax.rem(row + d, n), col)
        return (
            pltpu.make_async_remote_copy(
                src_ref=rg_ref.at[row], dst_ref=rg_ref.at[row], send_sem=r_send.at[d], recv_sem=r_recv.at[row],
                device_id=target, device_id_type=MESH,
            ),
            pltpu.make_async_remote_copy(
                src_ref=mask_ref, dst_ref=mr_ref.at[row], send_sem=mr_send.at[d], recv_sem=mr_recv.at[row],
                device_id=target, device_id_type=MESH,
            ),
        )

    for d in range(1, n):
        for copy in left_copies(d):
            copy.start()

    @pl.when(jnp.logical_not(own))
    def _():
        for copy in left_copies(0):
            copy.start()

    rg_ref[row] = project(norm_sj, wr_ref, br_ref, flat_sj_ref)
    for d in range(1, n):
        for copy in right_copies(d):
            copy.start()

    mr_ref[row] = mask_ref[...]

    @pl.when(own)
    def _():
        lg_ref[row] = left_own[...]
        ml_ref[row] = mask_ref[...]

    for d in range(1, n):
        for copy in left_copies(d) + right_copies(d):
            copy.wait_send()

    @pl.when(jnp.logical_not(own))
    def _():
        for copy in left_copies(0):
            copy.wait_send()

    def arrived(dst, slot, sem):
        pltpu.make_async_remote_copy(
            src_ref=dst.at[slot], dst_ref=dst.at[slot], send_sem=l_send.at[0], recv_sem=sem.at[slot],
            device_id=(grp, lax.rem(row + 1, n), col), device_id_type=MESH,
        ).wait_recv()

    for d in range(1, n):
        slot = lax.rem(row + d, n)
        arrived(rg_ref, slot, r_recv)
        arrived(mr_ref, slot, mr_recv)
        arrived(lg_ref, slot, l_recv)
        arrived(ml_ref, slot, ml_recv)

    @pl.when(jnp.logical_not(own))
    def _():
        arrived(lg_ref, row, l_recv)
        arrived(ml_ref, row, ml_recv)


def pair_kernel(
    seqs, res, lg_ref, rg_ref, ml_ref, mr_ref, wt_ref, shift_ref, out_ref, stage, right, left, outer, scale
):
    n, width, _ = rg_ref.shape
    block = out_ref.shape[0]
    step = pl.program_id(0)

    @pl.when(step == 0)
    def _():
        blank = jnp.zeros((width, LANES - res), jnp.float32)
        for k in range(n):
            for s in range(seqs):
                piece = rg_ref[k, :, s * res : (s + 1) * res].astype(jnp.float32)
                at = (k * seqs + s) * width
                stage[at : at + width, :] = jnp.concatenate([piece, blank], axis=1)
        for q in range(width):
            right[:, q * LANES : (q + 1) * LANES] = stage[pl.ds(q, n * seqs, stride=width), :].astype(
                jnp.bfloat16
            )
        count = lax.dot_general(
            ml_ref[...].reshape(n * seqs, LANES).astype(jnp.bfloat16),
            mr_ref[...].reshape(n * seqs, LANES).astype(jnp.bfloat16),
            (((0,), (0,)), ((), ())),
            preferred_element_type=jnp.float32,
        )
        scale[...] = 1.0 / jnp.maximum(count, 1.0)

    for i in range(block):
        left[i * width : (i + 1) * width, :] = jnp.concatenate(
            [lg_ref[k, :, i * seqs : (i + 1) * seqs] for k in range(n)], axis=1
        )

    wide = 2 * LANES

    def products(c, carry):
        at = pl.multiple_of(c * wide, wide)
        acc = jnp.dot(left[...], right[:, pl.ds(at, wide)], preferred_element_type=jnp.float32).astype(
            jnp.bfloat16
        )
        for h in range(2):
            low = pl.multiple_of((2 * c + h) * width, width)
            for i in range(block):
                outer[pl.ds(low, width), i * LANES : (i + 1) * LANES] = acc[
                    i * width : (i + 1) * width, h * LANES : (h + 1) * LANES
                ]
        return carry

    lax.fori_loop(0, width // 2, products, 0, unroll=2)

    shift = shift_ref[...]
    for c in range(block // 2):
        acc = jnp.dot(wt_ref[...], outer[:, c * wide : (c + 1) * wide], preferred_element_type=jnp.float32)
        for h in range(2):
            i = 2 * c + h
            one = (acc[:, h * LANES : (h + 1) * LANES] + shift) * scale[pl.ds(step * block + i, 1), :]
            out_ref[i] = one.T[:res].astype(jnp.bfloat16)


def local(n, x, occupancy, gain, bias, wl, bl, wr, br, wf, bf):
    seqs, res, feat = x.shape
    width = wl.shape[1]
    pair = wf.shape[1]
    tokens = seqs * res
    occ = occupancy.astype(jnp.float32)
    flat_sj = occ.reshape(1, tokens)
    flat_is = occ.T.reshape(1, tokens)
    mask = jnp.pad(occ, ((0, 0), (0, LANES - res)))
    whole = pl.BlockSpec(memory_space=pltpu.VMEM)
    dma = pltpu.SemaphoreType.DMA((n,))
    lg, rg, ml, mr = pl.pallas_call(
        functools.partial(exchange_kernel, n),
        out_shape=(
            jax.ShapeDtypeStruct((n, width, tokens), jnp.bfloat16),
            jax.ShapeDtypeStruct((n, width, tokens), jnp.bfloat16),
            jax.ShapeDtypeStruct((n, seqs, LANES), jnp.float32),
            jax.ShapeDtypeStruct((n, seqs, LANES), jnp.float32),
        ),
        in_specs=[whole] * 10,
        out_specs=(whole,) * 4,
        scratch_shapes=[
            pltpu.VMEM((feat // LANES, tokens, LANES), jnp.float32),
            pltpu.VMEM((feat // LANES, tokens, LANES), jnp.float32),
            pltpu.VMEM((width, tokens), jnp.bfloat16),
        ]
        + [dma] * 8,
        compiler_params=pltpu.CompilerParams(
            collective_id=0, has_side_effects=True, vmem_limit_bytes=VMEM_LIMIT
        ),
    )(
        x,
        gain.reshape(1, feat),
        bias.reshape(1, feat),
        wl.T,
        bl.reshape(width, 1),
        wr.T,
        br.reshape(width, 1),
        flat_sj,
        flat_is,
        mask,
    )
    wt = jnp.transpose(wf.reshape(width, width, pair), (2, 1, 0)).reshape(pair, width * width)
    block = 16
    depth = n * seqs

    def fixed(*shape):
        return pl.BlockSpec(shape, lambda b: (0,) * len(shape))

    return pl.pallas_call(
        functools.partial(pair_kernel, seqs, res),
        grid=(res // block,),
        out_shape=jax.ShapeDtypeStruct((res, res, pair), jnp.bfloat16),
        in_specs=[
            pl.BlockSpec((n, width, block * seqs), lambda b: (0, 0, b)),
            fixed(n, width, tokens),
            fixed(n, seqs, LANES),
            fixed(n, seqs, LANES),
            fixed(pair, width * width),
            fixed(pair, 1),
        ],
        out_specs=pl.BlockSpec((block, res, pair), lambda b: (b, 0, 0)),
        scratch_shapes=[
            pltpu.VMEM((depth * width, LANES), jnp.float32),
            pltpu.VMEM((depth, width * LANES), jnp.bfloat16),
            pltpu.VMEM((block * width, depth), jnp.bfloat16),
            pltpu.VMEM((width * width, block * LANES), jnp.bfloat16),
            pltpu.VMEM((LANES, LANES), jnp.float32),
        ],
        compiler_params=pltpu.CompilerParams(vmem_limit_bytes=VMEM_LIMIT),
    )(lg, rg, ml, mr, wt, bf.reshape(pair, 1))


def solution(mesh):
    placed = (P(("grp", "row"), "col", None), P(("grp", "row"), "col")) + (P(),) * 8
    return jax.shard_map(
        functools.partial(local, mesh.shape["row"]),
        mesh=mesh,
        in_specs=placed,
        out_specs=P(("grp", "row"), "col", None),
        check_vma=False,
    )
```

```python
import functools

import jax
import jax.numpy as jnp
from jax import lax
from jax.experimental import pallas as pl
from jax.experimental.pallas import tpu as pltpu
from jax.sharding import PartitionSpec as P

MESH = pl.DeviceIdType.MESH
LANES = 128
VMEM_LIMIT = 56 * 1024 * 1024


def column(line):
    size = line.shape[1]
    down = lax.broadcasted_iota(jnp.int32, (size, size), 0)
    across = lax.broadcasted_iota(jnp.int32, (size, size), 1)
    return jnp.sum(jnp.where(down == across, line, 0.0), axis=1, keepdims=True)


def exchange_kernel(
    n,
    x_ref,
    gain_ref,
    bias_ref,
    wl_ref,
    bl_ref,
    wr_ref,
    br_ref,
    occ_ref,
    wf_ref,
    lg_ref,
    rg_ref,
    ml_ref,
    mr_ref,
    wt_ref,
    norm_sj,
    norm_is,
    left_own,
    mask_ref,
    final_in,
    final_mid,
    l_send,
    l_recv,
    r_send,
    r_recv,
    ml_send,
    ml_recv,
    mr_send,
    mr_recv,
):
    seqs, res, feat = x_ref.shape
    halves = feat // LANES
    tokens = seqs * res
    grp = lax.axis_index("grp")
    row = lax.axis_index("row")
    col = lax.axis_index("col")
    own = row == col

    barrier = pltpu.get_barrier_semaphore()
    for d in range(1, n):
        pl.semaphore_signal(barrier, inc=1, device_id=(grp, lax.rem(row + d, n), col), device_id_type=MESH)
        pl.semaphore_signal(barrier, inc=1, device_id=(grp, lax.rem(row + d, n), row), device_id_type=MESH)

    @pl.when(jnp.logical_not(own))
    def _():
        pl.semaphore_signal(barrier, inc=1, device_id=(grp, row, row), device_id_type=MESH)

    gain = gain_ref[...]
    bias = bias_ref[...]
    occ = occ_ref[...].astype(jnp.float32)
    mask_ref[...] = jnp.concatenate([occ, jnp.zeros((seqs, LANES - res), jnp.float32)], axis=1)
    flat_sj = jnp.concatenate([occ[s : s + 1] for s in range(seqs)], axis=1)
    turned = mask_ref[...].T[:res]
    flat_is = jnp.concatenate([turned[i : i + 1] for i in range(res)], axis=1)

    def normalize(s, carry):
        e = x_ref[s].astype(jnp.float32)
        center = e - jnp.mean(e, axis=-1, keepdims=True)
        spread = jnp.mean(center * center, axis=-1, keepdims=True)
        v = center * lax.rsqrt(spread + 1e-05) * gain + bias
        at = pl.multiple_of(s * res, 8)
        for h in range(halves):
            norm_sj[h, pl.ds(at, res), :] = v[:, h * LANES : (h + 1) * LANES]
        return carry

    lax.fori_loop(0, seqs, normalize, 0)

    def reorder(i, carry):
        at = pl.multiple_of(i * seqs, 8)
        for h in range(halves):
            norm_is[h, pl.ds(at, seqs), :] = norm_sj[h, pl.ds(i, seqs, stride=res), :]
        return carry

    lax.fori_loop(0, res, reorder, 0, unroll=4)

    def project(src, w_ref, b_ref, flat):
        total = column(b_ref[...])
        acc = None
        for h in range(halves):
            part = lax.dot_general(
                w_ref[:, h * LANES : (h + 1) * LANES],
                src[h].astype(jnp.bfloat16),
                (((1,), (1,)), ((), ())),
                preferred_element_type=jnp.float32,
            )
            acc = part if acc is None else acc + part
        return ((acc + total) * flat).astype(jnp.bfloat16)

    left_own[...] = project(norm_is, wl_ref, bl_ref, flat_is)

    others = (n - 1) + n - own.astype(jnp.int32)
    pl.semaphore_wait(barrier, others)

    def left_copies(d):
        target = (grp, col, lax.rem(col + d, n))
        return (
            pltpu.make_async_remote_copy(
                src_ref=left_own, dst_ref=lg_ref.at[row], send_sem=l_send.at[d], recv_sem=l_recv.at[row],
                device_id=target, device_id_type=MESH,
            ),
            pltpu.make_async_remote_copy(
                src_ref=mask_ref, dst_ref=ml_ref.at[row], send_sem=ml_send.at[d], recv_sem=ml_recv.at[row],
                device_id=target, device_id_type=MESH,
            ),
        )

    def right_copies(d):
        target = (grp, lax.rem(row + d, n), col)
        return (
            pltpu.make_async_remote_copy(
                src_ref=rg_ref.at[row], dst_ref=rg_ref.at[row], send_sem=r_send.at[d], recv_sem=r_recv.at[row],
                device_id=target, device_id_type=MESH,
            ),
            pltpu.make_async_remote_copy(
                src_ref=mask_ref, dst_ref=mr_ref.at[row], send_sem=mr_send.at[d], recv_sem=mr_recv.at[row],
                device_id=target, device_id_type=MESH,
            ),
        )

    for d in range(1, n):
        for copy in left_copies(d):
            copy.start()

    @pl.when(jnp.logical_not(own))
    def _():
        for copy in left_copies(0):
            copy.start()

    rg_ref[row] = project(norm_sj, wr_ref, br_ref, flat_sj)
    for d in range(1, n):
        for copy in right_copies(d):
            copy.start()

    mr_ref[row] = mask_ref[...]

    @pl.when(own)
    def _():
        lg_ref[row] = left_own[...]
        ml_ref[row] = mask_ref[...]

    width = left_own.shape[0]
    final_in[...] = wf_ref[...].astype(jnp.float32)
    for q in range(width):
        final_mid[q * width : (q + 1) * width, :] = final_in[pl.ds(q, width, stride=width), :]
    for k in range(width * width // LANES):
        part = slice(k * LANES, (k + 1) * LANES)
        wt_ref[:, part] = final_mid[part, :].T.astype(jnp.bfloat16)

    for d in range(1, n):
        for copy in left_copies(d) + right_copies(d):
            copy.wait_send()

    @pl.when(jnp.logical_not(own))
    def _():
        for copy in left_copies(0):
            copy.wait_send()

    def arrived(dst, slot, sem):
        pltpu.make_async_remote_copy(
            src_ref=dst.at[slot], dst_ref=dst.at[slot], send_sem=l_send.at[0], recv_sem=sem.at[slot],
            device_id=(grp, lax.rem(row + 1, n), col), device_id_type=MESH,
        ).wait_recv()

    for d in range(1, n):
        slot = lax.rem(row + d, n)
        arrived(rg_ref, slot, r_recv)
        arrived(mr_ref, slot, mr_recv)
        arrived(lg_ref, slot, l_recv)
        arrived(ml_ref, slot, ml_recv)

    @pl.when(jnp.logical_not(own))
    def _():
        arrived(lg_ref, row, l_recv)
        arrived(ml_ref, row, ml_recv)


def pair_kernel(
    seqs, res, lg_ref, rg_ref, ml_ref, mr_ref, wt_ref, shift_ref, out_ref, stage, right, left, outer, scale, shift
):
    n, width, _ = rg_ref.shape
    block = out_ref.shape[0]
    step = pl.program_id(0)

    @pl.when(step == 0)
    def _():
        blank = jnp.zeros((width, LANES - res), jnp.float32)
        for k in range(n):
            for s in range(seqs):
                piece = rg_ref[k, :, s * res : (s + 1) * res].astype(jnp.float32)
                at = (k * seqs + s) * width
                stage[at : at + width, :] = jnp.concatenate([piece, blank], axis=1)
        for q in range(width):
            right[:, q * LANES : (q + 1) * LANES] = stage[pl.ds(q, n * seqs, stride=width), :].astype(
                jnp.bfloat16
            )
        count = lax.dot_general(
            ml_ref[...].reshape(n * seqs, LANES).astype(jnp.bfloat16),
            mr_ref[...].reshape(n * seqs, LANES).astype(jnp.bfloat16),
            (((0,), (0,)), ((), ())),
            preferred_element_type=jnp.float32,
        )
        scale[...] = 1.0 / jnp.maximum(count, 1.0)
        shift[...] = jnp.broadcast_to(column(shift_ref[...]), shift.shape)

    for i in range(block):
        left[i * width : (i + 1) * width, :] = jnp.concatenate(
            [lg_ref[k, :, i * seqs : (i + 1) * seqs] for k in range(n)], axis=1
        )

    wide = 2 * LANES

    def products(c, carry):
        at = pl.multiple_of(c * wide, wide)
        acc = jnp.dot(left[...], right[:, pl.ds(at, wide)], preferred_element_type=jnp.float32).astype(
            jnp.bfloat16
        )
        for h in range(2):
            low = pl.multiple_of((2 * c + h) * width, width)
            for i in range(block):
                outer[pl.ds(low, width), i * LANES : (i + 1) * LANES] = acc[
                    i * width : (i + 1) * width, h * LANES : (h + 1) * LANES
                ]
        return carry

    lax.fori_loop(0, width // 2, products, 0, unroll=True)

    moved = shift[...]
    for c in range(block // 2):
        acc = jnp.dot(wt_ref[...], outer[:, c * wide : (c + 1) * wide], preferred_element_type=jnp.float32)
        for h in range(2):
            i = 2 * c + h
            one = (acc[:, h * LANES : (h + 1) * LANES] + moved) * scale[pl.ds(step * block + i, 1), :]
            out_ref[i] = one.T[:res].astype(jnp.bfloat16)


def local(n, x, occupancy, gain, bias, wl, bl, wr, br, wf, bf):
    seqs, res, feat = x.shape
    width = wl.shape[1]
    pair = wf.shape[1]
    tokens = seqs * res
    whole = pl.BlockSpec(memory_space=pltpu.VMEM)
    dma = pltpu.SemaphoreType.DMA((n,))
    lg, rg, ml, mr, wt = pl.pallas_call(
        functools.partial(exchange_kernel, n),
        out_shape=(
            jax.ShapeDtypeStruct((n, width, tokens), jnp.bfloat16),
            jax.ShapeDtypeStruct((n, width, tokens), jnp.bfloat16),
            jax.ShapeDtypeStruct((n, seqs, LANES), jnp.float32),
            jax.ShapeDtypeStruct((n, seqs, LANES), jnp.float32),
            jax.ShapeDtypeStruct((pair, width * width), jnp.bfloat16),
        ),
        in_specs=[whole] * 9,
        out_specs=(whole,) * 5,
        scratch_shapes=[
            pltpu.VMEM((feat // LANES, tokens, LANES), jnp.float32),
            pltpu.VMEM((feat // LANES, tokens, LANES), jnp.float32),
            pltpu.VMEM((width, tokens), jnp.bfloat16),
            pltpu.VMEM((seqs, LANES), jnp.float32),
            pltpu.VMEM((width * width, pair), jnp.float32),
            pltpu.VMEM((width * width, pair), jnp.float32),
        ]
        + [dma] * 8,
        compiler_params=pltpu.CompilerParams(
            collective_id=0, has_side_effects=True, vmem_limit_bytes=VMEM_LIMIT
        ),
    )(
        x,
        gain.reshape(1, feat),
        bias.reshape(1, feat),
        wl.T,
        bl.reshape(1, width),
        wr.T,
        br.reshape(1, width),
        occupancy,
        wf,
    )
    block = 16
    depth = n * seqs

    def fixed(*shape):
        return pl.BlockSpec(shape, lambda b: (0,) * len(shape))

    return pl.pallas_call(
        functools.partial(pair_kernel, seqs, res),
        grid=(res // block,),
        out_shape=jax.ShapeDtypeStruct((res, res, pair), jnp.bfloat16),
        in_specs=[
            pl.BlockSpec((n, width, block * seqs), lambda b: (0, 0, b)),
            fixed(n, width, tokens),
            fixed(n, seqs, LANES),
            fixed(n, seqs, LANES),
            fixed(pair, width * width),
            fixed(1, pair),
        ],
        out_specs=pl.BlockSpec((block, res, pair), lambda b: (b, 0, 0)),
        scratch_shapes=[
            pltpu.VMEM((depth * width, LANES), jnp.float32),
            pltpu.VMEM((depth, width * LANES), jnp.bfloat16),
            pltpu.VMEM((block * width, depth), jnp.bfloat16),
            pltpu.VMEM((width * width, block * LANES), jnp.bfloat16),
            pltpu.VMEM((LANES, LANES), jnp.float32),
            pltpu.VMEM((pair, LANES), jnp.float32),
        ],
        compiler_params=pltpu.CompilerParams(vmem_limit_bytes=VMEM_LIMIT),
    )(lg, rg, ml, mr, wt, bf.reshape(1, pair))


def solution(mesh):
    placed = (P(("grp", "row"), "col", None), P(("grp", "row"), "col")) + (P(),) * 8
    return jax.shard_map(
        functools.partial(local, mesh.shape["row"]),
        mesh=mesh,
        in_specs=placed,
        out_specs=P(("grp", "row"), "col", None),
        check_vma=False,
    )
```

```python
import functools

import jax
import jax.numpy as jnp
from jax import lax
from jax.experimental import pallas as pl
from jax.experimental.pallas import tpu as pltpu
from jax.sharding import PartitionSpec as P

MESH = pl.DeviceIdType.MESH
LANES = 128
GROUP = 8
VMEM_LIMIT = 56 * 1024 * 1024


def column(line):
    size = line.shape[1]
    down = lax.broadcasted_iota(jnp.int32, (size, size), 0)
    across = lax.broadcasted_iota(jnp.int32, (size, size), 1)
    return jnp.sum(jnp.where(down == across, line, 0.0), axis=1, keepdims=True)


def exchange_kernel(
    n,
    x_ref,
    gain_ref,
    bias_ref,
    wl_ref,
    bl_ref,
    wr_ref,
    br_ref,
    occ_ref,
    wf_ref,
    lg_ref,
    rg_ref,
    ml_ref,
    mr_ref,
    wt_ref,
    norm_sj,
    norm_is,
    left_own,
    mask_ref,
    final_in,
    final_mid,
    l_send,
    l_recv,
    r_send,
    r_recv,
    ml_send,
    ml_recv,
    mr_send,
    mr_recv,
):
    seqs, res, feat = x_ref.shape
    halves = feat // LANES
    groups = seqs // GROUP
    chunk = GROUP * res
    tokens = seqs * res
    grp = lax.axis_index("grp")
    row = lax.axis_index("row")
    col = lax.axis_index("col")
    own = row == col

    barrier = pltpu.get_barrier_semaphore()
    for d in range(1, n):
        pl.semaphore_signal(barrier, inc=1, device_id=(grp, lax.rem(row + d, n), col), device_id_type=MESH)
        pl.semaphore_signal(barrier, inc=1, device_id=(grp, lax.rem(row + d, n), row), device_id_type=MESH)

    @pl.when(jnp.logical_not(own))
    def _():
        pl.semaphore_signal(barrier, inc=1, device_id=(grp, row, row), device_id_type=MESH)

    gain = gain_ref[...]
    bias = bias_ref[...]
    occ = occ_ref[...].astype(jnp.float32)
    mask_ref[...] = jnp.concatenate([occ, jnp.zeros((seqs, LANES - res), jnp.float32)], axis=1)
    flat_sj = jnp.concatenate([occ[s : s + 1] for s in range(seqs)], axis=1)
    turned = mask_ref[...].T[:res]
    flat_is = jnp.concatenate([turned[i : i + 1] for i in range(res)], axis=1)

    def normalize(s, carry):
        e = x_ref[s].astype(jnp.float32)
        center = e - jnp.mean(e, axis=-1, keepdims=True)
        spread = jnp.mean(center * center, axis=-1, keepdims=True)
        v = center * lax.rsqrt(spread + 1e-05) * gain + bias
        at = pl.multiple_of(s * res, 8)
        for h in range(halves):
            norm_sj[h, pl.ds(at, res), :] = v[:, h * LANES : (h + 1) * LANES]
        return carry

    def project(src, low, size, w_ref, add, flat):
        acc = None
        for h in range(halves):
            part = lax.dot_general(
                w_ref[:, h * LANES : (h + 1) * LANES],
                src[h, low : low + size].astype(jnp.bfloat16),
                (((1,), (1,)), ((), ())),
                preferred_element_type=jnp.float32,
            )
            acc = part if acc is None else acc + part
        return ((acc + add) * flat).astype(jnp.bfloat16)

    add_left = column(bl_ref[...])
    add_right = column(br_ref[...])

    others = (n - 1) + n - own.astype(jnp.int32)
    pl.semaphore_wait(barrier, others)

    def left_copy(d):
        return pltpu.make_async_remote_copy(
            src_ref=left_own, dst_ref=lg_ref.at[row], send_sem=l_send.at[d], recv_sem=l_recv.at[row],
            device_id=(grp, col, lax.rem(col + d, n)), device_id_type=MESH,
        )

    def left_mask_copy(d):
        return pltpu.make_async_remote_copy(
            src_ref=mask_ref, dst_ref=ml_ref.at[row], send_sem=ml_send.at[d], recv_sem=ml_recv.at[row],
            device_id=(grp, col, lax.rem(col + d, n)), device_id_type=MESH,
        )

    def right_copy(d, g):
        piece = rg_ref.at[row, :, pl.ds(g * chunk, chunk)]
        return pltpu.make_async_remote_copy(
            src_ref=piece, dst_ref=piece, send_sem=r_send.at[d, g], recv_sem=r_recv.at[row, g],
            device_id=(grp, lax.rem(row + d, n), col), device_id_type=MESH,
        )

    def right_mask_copy(d):
        return pltpu.make_async_remote_copy(
            src_ref=mask_ref, dst_ref=mr_ref.at[row], send_sem=mr_send.at[d], recv_sem=mr_recv.at[row],
            device_id=(grp, lax.rem(row + d, n), col), device_id_type=MESH,
        )

    for d in range(1, n):
        left_mask_copy(d).start()
        right_mask_copy(d).start()

    @pl.when(jnp.logical_not(own))
    def _():
        left_mask_copy(0).start()

    for g in range(groups):
        lax.fori_loop(g * GROUP, (g + 1) * GROUP, normalize, 0, unroll=4)
        part = slice(g * chunk, (g + 1) * chunk)
        rg_ref[row, :, part] = project(norm_sj, g * chunk, chunk, wr_ref, add_right, flat_sj[:, part])
        for d in range(1, n):
            right_copy(d, g).start()

    def reorder(i, carry):
        at = pl.multiple_of(i * seqs, 8)
        for h in range(halves):
            norm_is[h, pl.ds(at, seqs), :] = norm_sj[h, pl.ds(i, seqs, stride=res), :]
        return carry

    lax.fori_loop(0, res, reorder, 0, unroll=4)

    left_own[...] = project(norm_is, 0, tokens, wl_ref, add_left, flat_is)
    for d in range(n - 1, 0, -1):
        left_copy(d).start()

    @pl.when(jnp.logical_not(own))
    def _():
        left_copy(0).start()

    mr_ref[row] = mask_ref[...]

    @pl.when(own)
    def _():
        lg_ref[row] = left_own[...]
        ml_ref[row] = mask_ref[...]

    width = left_own.shape[0]
    final_in[...] = wf_ref[...].astype(jnp.float32)
    for q in range(width):
        final_mid[q * width : (q + 1) * width, :] = final_in[pl.ds(q, width, stride=width), :]
    for k in range(width * width // LANES):
        part = slice(k * LANES, (k + 1) * LANES)
        wt_ref[:, part] = final_mid[part, :].T.astype(jnp.bfloat16)

    for d in range(1, n):
        left_mask_copy(d).wait_send()
        right_mask_copy(d).wait_send()
        left_copy(d).wait_send()
        for g in range(groups):
            right_copy(d, g).wait_send()

    @pl.when(jnp.logical_not(own))
    def _():
        left_mask_copy(0).wait_send()
        left_copy(0).wait_send()

    def arrived(dst, sem):
        pltpu.make_async_remote_copy(
            src_ref=dst, dst_ref=dst, send_sem=l_send.at[0], recv_sem=sem,
            device_id=(grp, lax.rem(row + 1, n), col), device_id_type=MESH,
        ).wait_recv()

    for d in range(1, n):
        slot = lax.rem(row + d, n)
        arrived(mr_ref.at[slot], mr_recv.at[slot])
        arrived(ml_ref.at[slot], ml_recv.at[slot])
        for g in range(groups):
            arrived(rg_ref.at[slot, :, pl.ds(g * chunk, chunk)], r_recv.at[slot, g])
        arrived(lg_ref.at[slot], l_recv.at[slot])

    @pl.when(jnp.logical_not(own))
    def _():
        arrived(lg_ref.at[row], l_recv.at[row])
        arrived(ml_ref.at[row], ml_recv.at[row])


def pair_kernel(
    seqs, res, lg_ref, rg_ref, ml_ref, mr_ref, wt_ref, shift_ref, out_ref, stage, right, left, outer, scale, shift
):
    n, width, _ = rg_ref.shape
    block = out_ref.shape[0]
    step = pl.program_id(0)

    @pl.when(step == 0)
    def _():
        blank = jnp.zeros((width, LANES - res), jnp.float32)
        for k in range(n):
            for s in range(seqs):
                piece = rg_ref[k, :, s * res : (s + 1) * res].astype(jnp.float32)
                at = (k * seqs + s) * width
                stage[at : at + width, :] = jnp.concatenate([piece, blank], axis=1)
        for q in range(width):
            right[:, q * LANES : (q + 1) * LANES] = stage[pl.ds(q, n * seqs, stride=width), :].astype(
                jnp.bfloat16
            )
        count = lax.dot_general(
            ml_ref[...].reshape(n * seqs, LANES).astype(jnp.bfloat16),
            mr_ref[...].reshape(n * seqs, LANES).astype(jnp.bfloat16),
            (((0,), (0,)), ((), ())),
            preferred_element_type=jnp.float32,
        )
        scale[...] = 1.0 / jnp.maximum(count, 1.0)
        shift[...] = jnp.broadcast_to(column(shift_ref[...]), shift.shape)

    for i in range(block):
        left[i * width : (i + 1) * width, :] = jnp.concatenate(
            [lg_ref[k, :, i * seqs : (i + 1) * seqs] for k in range(n)], axis=1
        )

    wide = 2 * LANES

    def products(c, carry):
        at = pl.multiple_of(c * wide, wide)
        acc = jnp.dot(left[...], right[:, pl.ds(at, wide)], preferred_element_type=jnp.float32).astype(
            jnp.bfloat16
        )
        for h in range(2):
            low = pl.multiple_of((2 * c + h) * width, width)
            for i in range(block):
                outer[pl.ds(low, width), i * LANES : (i + 1) * LANES] = acc[
                    i * width : (i + 1) * width, h * LANES : (h + 1) * LANES
                ]
        return carry

    lax.fori_loop(0, width // 2, products, 0, unroll=True)

    moved = shift[...]
    for c in range(block // 2):
        acc = jnp.dot(wt_ref[...], outer[:, c * wide : (c + 1) * wide], preferred_element_type=jnp.float32)
        for h in range(2):
            i = 2 * c + h
            one = (acc[:, h * LANES : (h + 1) * LANES] + moved) * scale[pl.ds(step * block + i, 1), :]
            out_ref[i] = one.T[:res].astype(jnp.bfloat16)


def local(n, x, occupancy, gain, bias, wl, bl, wr, br, wf, bf):
    seqs, res, feat = x.shape
    width = wl.shape[1]
    pair = wf.shape[1]
    tokens = seqs * res
    whole = pl.BlockSpec(memory_space=pltpu.VMEM)
    dma = pltpu.SemaphoreType.DMA((n,))
    lg, rg, ml, mr, wt = pl.pallas_call(
        functools.partial(exchange_kernel, n),
        out_shape=(
            jax.ShapeDtypeStruct((n, width, tokens), jnp.bfloat16),
            jax.ShapeDtypeStruct((n, width, tokens), jnp.bfloat16),
            jax.ShapeDtypeStruct((n, seqs, LANES), jnp.float32),
            jax.ShapeDtypeStruct((n, seqs, LANES), jnp.float32),
            jax.ShapeDtypeStruct((pair, width * width), jnp.bfloat16),
        ),
        in_specs=[whole] * 9,
        out_specs=(whole,) * 5,
        scratch_shapes=[
            pltpu.VMEM((feat // LANES, tokens, LANES), jnp.float32),
            pltpu.VMEM((feat // LANES, tokens, LANES), jnp.float32),
            pltpu.VMEM((width, tokens), jnp.bfloat16),
            pltpu.VMEM((seqs, LANES), jnp.float32),
            pltpu.VMEM((width * width, pair), jnp.float32),
            pltpu.VMEM((width * width, pair), jnp.float32),
        ]
        + [dma] * 2
        + [pltpu.SemaphoreType.DMA((n, seqs // GROUP))] * 2
        + [dma] * 4,
        compiler_params=pltpu.CompilerParams(
            collective_id=0, has_side_effects=True, vmem_limit_bytes=VMEM_LIMIT
        ),
    )(
        x,
        gain.reshape(1, feat),
        bias.reshape(1, feat),
        wl.T,
        bl.reshape(1, width),
        wr.T,
        br.reshape(1, width),
        occupancy,
        wf,
    )
    block = 16
    depth = n * seqs

    def fixed(*shape):
        return pl.BlockSpec(shape, lambda b: (0,) * len(shape))

    return pl.pallas_call(
        functools.partial(pair_kernel, seqs, res),
        grid=(res // block,),
        out_shape=jax.ShapeDtypeStruct((res, res, pair), jnp.bfloat16),
        in_specs=[
            pl.BlockSpec((n, width, block * seqs), lambda b: (0, 0, b)),
            fixed(n, width, tokens),
            fixed(n, seqs, LANES),
            fixed(n, seqs, LANES),
            fixed(pair, width * width),
            fixed(1, pair),
        ],
        out_specs=pl.BlockSpec((block, res, pair), lambda b: (b, 0, 0)),
        scratch_shapes=[
            pltpu.VMEM((depth * width, LANES), jnp.float32),
            pltpu.VMEM((depth, width * LANES), jnp.bfloat16),
            pltpu.VMEM((block * width, depth), jnp.bfloat16),
            pltpu.VMEM((width * width, block * LANES), jnp.bfloat16),
            pltpu.VMEM((LANES, LANES), jnp.float32),
            pltpu.VMEM((pair, LANES), jnp.float32),
        ],
        compiler_params=pltpu.CompilerParams(vmem_limit_bytes=VMEM_LIMIT),
    )(lg, rg, ml, mr, wt, bf.reshape(1, pair))


def solution(mesh):
    placed = (P(("grp", "row"), "col", None), P(("grp", "row"), "col")) + (P(),) * 8
    return jax.shard_map(
        functools.partial(local, mesh.shape["row"]),
        mesh=mesh,
        in_specs=placed,
        out_specs=P(("grp", "row"), "col", None),
        check_vma=False,
    )
```

```python
import functools

import jax
import jax.numpy as jnp
from jax import lax
from jax.experimental import pallas as pl
from jax.experimental.pallas import tpu as pltpu
from jax.sharding import PartitionSpec as P

MESH = pl.DeviceIdType.MESH
LANES = 128
GROUP = 8
VMEM_LIMIT = 56 * 1024 * 1024


def column(line):
    size = line.shape[1]
    down = lax.broadcasted_iota(jnp.int32, (size, size), 0)
    across = lax.broadcasted_iota(jnp.int32, (size, size), 1)
    return jnp.sum(jnp.where(down == across, line, 0.0), axis=1, keepdims=True)


def exchange_kernel(
    n,
    x_ref,
    gain_ref,
    bias_ref,
    wl_ref,
    bl_ref,
    wr_ref,
    br_ref,
    occ_ref,
    wf_ref,
    lg_ref,
    rg_ref,
    ml_ref,
    mr_ref,
    wt_ref,
    norm_sj,
    norm_is,
    line,
    mask_ref,
    final_in,
    final_mid,
    z_send,
    z_recv,
    l_send,
    l_recv,
    r_send,
    r_recv,
    ml_send,
    ml_recv,
    mr_send,
    mr_recv,
):
    seqs, res, feat = x_ref.shape
    halves = feat // LANES
    groups = seqs // GROUP
    chunk = GROUP * res
    tokens = seqs * res
    grp = lax.axis_index("grp")
    row = lax.axis_index("row")
    col = lax.axis_index("col")
    own = row == col

    barrier = pltpu.get_barrier_semaphore()
    for d in range(1, n):
        pl.semaphore_signal(barrier, inc=1, device_id=(grp, lax.rem(row + d, n), col), device_id_type=MESH)
        pl.semaphore_signal(barrier, inc=1, device_id=(grp, lax.rem(row + d, n), row), device_id_type=MESH)

    @pl.when(jnp.logical_not(own))
    def _():
        pl.semaphore_signal(barrier, inc=1, device_id=(grp, row, row), device_id_type=MESH)

    def inside(place):
        return jnp.logical_and(place >= 0, place < n)

    for way in (-1, 1):

        @pl.when(inside(col + way))
        def _():
            pl.semaphore_signal(barrier, inc=1, device_id=(grp, row, col + way), device_id_type=MESH)

    gain = gain_ref[...]
    bias = bias_ref[...]
    occ = occ_ref[...].astype(jnp.float32)
    mask_ref[...] = jnp.concatenate([occ, jnp.zeros((seqs, LANES - res), jnp.float32)], axis=1)
    flat_sj = jnp.concatenate([occ[s : s + 1] for s in range(seqs)], axis=1)
    turned = mask_ref[...].T[:res]
    flat_is = jnp.concatenate([turned[i : i + 1] for i in range(res)], axis=1)

    def normalize(s, carry):
        e = x_ref[s].astype(jnp.float32)
        center = e - jnp.mean(e, axis=-1, keepdims=True)
        spread = jnp.mean(center * center, axis=-1, keepdims=True)
        v = center * lax.rsqrt(spread + 1e-05) * gain + bias
        at = pl.multiple_of(s * res, 8)
        for h in range(halves):
            norm_sj[h, pl.ds(at, res), :] = v[:, h * LANES : (h + 1) * LANES]
        return carry

    def project(src, low, size, w_ref, add, flat):
        acc = None
        for h in range(halves):
            part = lax.dot_general(
                w_ref[:, h * LANES : (h + 1) * LANES],
                src[h, low : low + size].astype(jnp.bfloat16),
                (((1,), (1,)), ((), ())),
                preferred_element_type=jnp.float32,
            )
            acc = part if acc is None else acc + part
        return ((acc + add) * flat).astype(jnp.bfloat16)

    add_left = column(bl_ref[...])
    add_right = column(br_ref[...])

    others = (n - 1) + n - own.astype(jnp.int32) + (col > 0).astype(jnp.int32) + (col < n - 1).astype(jnp.int32)
    pl.semaphore_wait(barrier, others)

    def hop_copy(src, way):
        return pltpu.make_async_remote_copy(
            src_ref=line.at[src], dst_ref=line.at[src], send_sem=z_send.at[(way + 1) // 2, src], recv_sem=z_recv.at[src],
            device_id=(grp, row, col + way), device_id_type=MESH,
        )

    def left_copy(src):
        return pltpu.make_async_remote_copy(
            src_ref=line.at[src], dst_ref=lg_ref.at[row], send_sem=l_send.at[src], recv_sem=l_recv.at[row],
            device_id=(grp, src, col), device_id_type=MESH,
        )

    def left_mask_copy(d):
        return pltpu.make_async_remote_copy(
            src_ref=mask_ref, dst_ref=ml_ref.at[row], send_sem=ml_send.at[d], recv_sem=ml_recv.at[row],
            device_id=(grp, col, lax.rem(col + d, n)), device_id_type=MESH,
        )

    def right_copy(d, g):
        piece = rg_ref.at[row, :, pl.ds(g * chunk, chunk)]
        return pltpu.make_async_remote_copy(
            src_ref=piece, dst_ref=piece, send_sem=r_send.at[d, g], recv_sem=r_recv.at[row, g],
            device_id=(grp, lax.rem(row + d, n), col), device_id_type=MESH,
        )

    def right_mask_copy(d):
        return pltpu.make_async_remote_copy(
            src_ref=mask_ref, dst_ref=mr_ref.at[row], send_sem=mr_send.at[d], recv_sem=mr_recv.at[row],
            device_id=(grp, lax.rem(row + d, n), col), device_id_type=MESH,
        )

    for d in range(1, n):
        left_mask_copy(d).start()
        right_mask_copy(d).start()

    @pl.when(jnp.logical_not(own))
    def _():
        left_mask_copy(0).start()

    for g in range(groups):
        lax.fori_loop(g * GROUP, (g + 1) * GROUP, normalize, 0, unroll=4)
        part = slice(g * chunk, (g + 1) * chunk)
        rg_ref[row, :, part] = project(norm_sj, g * chunk, chunk, wr_ref, add_right, flat_sj[:, part])
        for d in range(1, n):
            right_copy(d, g).start()

    def reorder(i, carry):
        at = pl.multiple_of(i * seqs, 8)
        for h in range(halves):
            norm_is[h, pl.ds(at, seqs), :] = norm_sj[h, pl.ds(i, seqs, stride=res), :]
        return carry

    lax.fori_loop(0, res, reorder, 0, unroll=4)

    line[col] = project(norm_is, 0, tokens, wl_ref, add_left, flat_is)
    for way in (-1, 1):

        @pl.when(inside(col + way))
        def _():
            hop_copy(col, way).start()

    @pl.when(jnp.logical_not(own))
    def _():
        left_copy(col).start()

    mr_ref[row] = mask_ref[...]

    @pl.when(own)
    def _():
        lg_ref[row] = line[col]
        ml_ref[row] = mask_ref[...]

    width = line.shape[1]
    final_in[...] = wf_ref[...].astype(jnp.float32)
    for q in range(width):
        final_mid[q * width : (q + 1) * width, :] = final_in[pl.ds(q, width, stride=width), :]
    for k in range(width * width // LANES):
        part = slice(k * LANES, (k + 1) * LANES)
        wt_ref[:, part] = final_mid[part, :].T.astype(jnp.bfloat16)

    def arrived(dst, sem):
        pltpu.make_async_remote_copy(
            src_ref=dst, dst_ref=dst, send_sem=l_send.at[0], recv_sem=sem,
            device_id=(grp, lax.rem(row + 1, n), col), device_id_type=MESH,
        ).wait_recv()

    for h in range(1, n):
        for way in (-1, 1):
            src = col - way * h

            @pl.when(inside(src))
            def _():
                arrived(line.at[src], z_recv.at[src])

                @pl.when(inside(col + way))
                def _():
                    hop_copy(src, way).start()

                @pl.when(src != row)
                def _():
                    left_copy(src).start()

                @pl.when(src == row)
                def _():
                    lg_ref[row] = line[src]

    for h in range(1, n):
        for way in (-1, 1):
            src = col - way * h

            @pl.when(jnp.logical_and(inside(src), inside(col + way)))
            def _():
                hop_copy(src, way).wait_send()

            @pl.when(jnp.logical_and(inside(src), src != row))
            def _():
                left_copy(src).wait_send()

    for way in (-1, 1):

        @pl.when(inside(col + way))
        def _():
            hop_copy(col, way).wait_send()

    for d in range(1, n):
        left_mask_copy(d).wait_send()
        right_mask_copy(d).wait_send()
        for g in range(groups):
            right_copy(d, g).wait_send()

    @pl.when(jnp.logical_not(own))
    def _():
        left_mask_copy(0).wait_send()
        left_copy(col).wait_send()

    for d in range(1, n):
        slot = lax.rem(row + d, n)
        arrived(mr_ref.at[slot], mr_recv.at[slot])
        arrived(ml_ref.at[slot], ml_recv.at[slot])
        for g in range(groups):
            arrived(rg_ref.at[slot, :, pl.ds(g * chunk, chunk)], r_recv.at[slot, g])
        arrived(lg_ref.at[slot], l_recv.at[slot])

    @pl.when(jnp.logical_not(own))
    def _():
        arrived(ml_ref.at[row], ml_recv.at[row])


def pair_kernel(
    seqs, res, lg_ref, rg_ref, ml_ref, mr_ref, wt_ref, shift_ref, out_ref, stage, right, left, outer, scale, shift
):
    n, width, _ = rg_ref.shape
    block = out_ref.shape[0]
    step = pl.program_id(0)

    @pl.when(step == 0)
    def _():
        blank = jnp.zeros((width, LANES - res), jnp.float32)
        for k in range(n):
            for s in range(seqs):
                piece = rg_ref[k, :, s * res : (s + 1) * res].astype(jnp.float32)
                at = (k * seqs + s) * width
                stage[at : at + width, :] = jnp.concatenate([piece, blank], axis=1)
        for q in range(width):
            right[:, q * LANES : (q + 1) * LANES] = stage[pl.ds(q, n * seqs, stride=width), :].astype(
                jnp.bfloat16
            )
        count = lax.dot_general(
            ml_ref[...].reshape(n * seqs, LANES).astype(jnp.bfloat16),
            mr_ref[...].reshape(n * seqs, LANES).astype(jnp.bfloat16),
            (((0,), (0,)), ((), ())),
            preferred_element_type=jnp.float32,
        )
        scale[...] = 1.0 / jnp.maximum(count, 1.0)
        shift[...] = jnp.broadcast_to(column(shift_ref[...]), shift.shape)

    for i in range(block):
        left[i * width : (i + 1) * width, :] = jnp.concatenate(
            [lg_ref[k, :, i * seqs : (i + 1) * seqs] for k in range(n)], axis=1
        )

    wide = 2 * LANES

    def products(c, carry):
        at = pl.multiple_of(c * wide, wide)
        acc = jnp.dot(left[...], right[:, pl.ds(at, wide)], preferred_element_type=jnp.float32).astype(
            jnp.bfloat16
        )
        for h in range(2):
            low = pl.multiple_of((2 * c + h) * width, width)
            for i in range(block):
                outer[pl.ds(low, width), i * LANES : (i + 1) * LANES] = acc[
                    i * width : (i + 1) * width, h * LANES : (h + 1) * LANES
                ]
        return carry

    lax.fori_loop(0, width // 2, products, 0, unroll=True)

    moved = shift[...]
    for c in range(block // 2):
        acc = jnp.dot(wt_ref[...], outer[:, c * wide : (c + 1) * wide], preferred_element_type=jnp.float32)
        for h in range(2):
            i = 2 * c + h
            one = (acc[:, h * LANES : (h + 1) * LANES] + moved) * scale[pl.ds(step * block + i, 1), :]
            out_ref[i] = one.T[:res].astype(jnp.bfloat16)


def local(n, x, occupancy, gain, bias, wl, bl, wr, br, wf, bf):
    seqs, res, feat = x.shape
    width = wl.shape[1]
    pair = wf.shape[1]
    tokens = seqs * res
    whole = pl.BlockSpec(memory_space=pltpu.VMEM)
    dma = pltpu.SemaphoreType.DMA((n,))
    lg, rg, ml, mr, wt = pl.pallas_call(
        functools.partial(exchange_kernel, n),
        out_shape=(
            jax.ShapeDtypeStruct((n, width, tokens), jnp.bfloat16),
            jax.ShapeDtypeStruct((n, width, tokens), jnp.bfloat16),
            jax.ShapeDtypeStruct((n, seqs, LANES), jnp.float32),
            jax.ShapeDtypeStruct((n, seqs, LANES), jnp.float32),
            jax.ShapeDtypeStruct((pair, width * width), jnp.bfloat16),
        ),
        in_specs=[whole] * 9,
        out_specs=(whole,) * 5,
        scratch_shapes=[
            pltpu.VMEM((feat // LANES, tokens, LANES), jnp.float32),
            pltpu.VMEM((feat // LANES, tokens, LANES), jnp.float32),
            pltpu.VMEM((n, width, tokens), jnp.bfloat16),
            pltpu.VMEM((seqs, LANES), jnp.float32),
            pltpu.VMEM((width * width, pair), jnp.float32),
            pltpu.VMEM((width * width, pair), jnp.float32),
        ]
        + [pltpu.SemaphoreType.DMA((2, n)), dma]
        + [dma] * 2
        + [pltpu.SemaphoreType.DMA((n, seqs // GROUP))] * 2
        + [dma] * 4,
        compiler_params=pltpu.CompilerParams(
            collective_id=0, has_side_effects=True, vmem_limit_bytes=VMEM_LIMIT
        ),
    )(
        x,
        gain.reshape(1, feat),
        bias.reshape(1, feat),
        wl.T,
        bl.reshape(1, width),
        wr.T,
        br.reshape(1, width),
        occupancy,
        wf,
    )
    block = 16
    depth = n * seqs

    def fixed(*shape):
        return pl.BlockSpec(shape, lambda b: (0,) * len(shape))

    return pl.pallas_call(
        functools.partial(pair_kernel, seqs, res),
        grid=(res // block,),
        out_shape=jax.ShapeDtypeStruct((res, res, pair), jnp.bfloat16),
        in_specs=[
            pl.BlockSpec((n, width, block * seqs), lambda b: (0, 0, b)),
            fixed(n, width, tokens),
            fixed(n, seqs, LANES),
            fixed(n, seqs, LANES),
            fixed(pair, width * width),
            fixed(1, pair),
        ],
        out_specs=pl.BlockSpec((block, res, pair), lambda b: (b, 0, 0)),
        scratch_shapes=[
            pltpu.VMEM((depth * width, LANES), jnp.float32),
            pltpu.VMEM((depth, width * LANES), jnp.bfloat16),
            pltpu.VMEM((block * width, depth), jnp.bfloat16),
            pltpu.VMEM((width * width, block * LANES), jnp.bfloat16),
            pltpu.VMEM((LANES, LANES), jnp.float32),
            pltpu.VMEM((pair, LANES), jnp.float32),
        ],
        compiler_params=pltpu.CompilerParams(vmem_limit_bytes=VMEM_LIMIT),
    )(lg, rg, ml, mr, wt, bf.reshape(1, pair))


def solution(mesh):
    placed = (P(("grp", "row"), "col", None), P(("grp", "row"), "col")) + (P(),) * 8
    return jax.shard_map(
        functools.partial(local, mesh.shape["row"]),
        mesh=mesh,
        in_specs=placed,
        out_specs=P(("grp", "row"), "col", None),
        check_vma=False,
    )
```

```python
import functools

import jax
import jax.numpy as jnp
from jax import lax
from jax.experimental import pallas as pl
from jax.experimental.pallas import tpu as pltpu
from jax.sharding import PartitionSpec as P

MESH = pl.DeviceIdType.MESH
LANES = 128
GROUP = 8
VMEM_LIMIT = 56 * 1024 * 1024


def column(line):
    size = line.shape[1]
    down = lax.broadcasted_iota(jnp.int32, (size, size), 0)
    across = lax.broadcasted_iota(jnp.int32, (size, size), 1)
    return jnp.sum(jnp.where(down == across, line, 0.0), axis=1, keepdims=True)


def exchange_kernel(
    n,
    x_ref,
    gain_ref,
    bias_ref,
    wl_ref,
    bl_ref,
    wr_ref,
    br_ref,
    occ_ref,
    wf_ref,
    lg_ref,
    rg_ref,
    ml_ref,
    mr_ref,
    wt_ref,
    norm_sj,
    norm_is,
    left_own,
    mask_ref,
    final_in,
    final_mid,
    l_send,
    l_recv,
    r_send,
    r_recv,
    s_send,
    ml_send,
    ml_recv,
    mr_send,
    mr_recv,
):
    seqs, res, feat = x_ref.shape
    halves = feat // LANES
    groups = seqs // GROUP
    chunk = GROUP * res
    tokens = seqs * res
    grp = lax.axis_index("grp")
    row = lax.axis_index("row")
    col = lax.axis_index("col")
    own = row == col
    sibling = row + 1 - 2 * lax.rem(row, 2)

    barrier = pltpu.get_barrier_semaphore()
    for d in range(1, n):
        pl.semaphore_signal(barrier, inc=1, device_id=(grp, lax.rem(row + d, n), col), device_id_type=MESH)
        pl.semaphore_signal(barrier, inc=1, device_id=(grp, lax.rem(row + d, n), row), device_id_type=MESH)

    @pl.when(jnp.logical_not(own))
    def _():
        pl.semaphore_signal(barrier, inc=1, device_id=(grp, row, row), device_id_type=MESH)

    gain = gain_ref[...]
    bias = bias_ref[...]
    occ = occ_ref[...].astype(jnp.float32)
    mask_ref[...] = jnp.concatenate([occ, jnp.zeros((seqs, LANES - res), jnp.float32)], axis=1)
    flat_sj = jnp.concatenate([occ[s : s + 1] for s in range(seqs)], axis=1)
    turned = mask_ref[...].T[:res]
    flat_is = jnp.concatenate([turned[i : i + 1] for i in range(res)], axis=1)

    def normalize(s, carry):
        e = x_ref[s].astype(jnp.float32)
        center = e - jnp.mean(e, axis=-1, keepdims=True)
        spread = jnp.mean(center * center, axis=-1, keepdims=True)
        v = center * lax.rsqrt(spread + 1e-05) * gain + bias
        at = pl.multiple_of(s * res, 8)
        for h in range(halves):
            norm_sj[h, pl.ds(at, res), :] = v[:, h * LANES : (h + 1) * LANES]
        return carry

    def project(src, low, size, w_ref, add, flat):
        acc = None
        for h in range(halves):
            part = lax.dot_general(
                w_ref[:, h * LANES : (h + 1) * LANES],
                src[h, low : low + size].astype(jnp.bfloat16),
                (((1,), (1,)), ((), ())),
                preferred_element_type=jnp.float32,
            )
            acc = part if acc is None else acc + part
        return ((acc + add) * flat).astype(jnp.bfloat16)

    add_left = column(bl_ref[...])
    add_right = column(br_ref[...])

    others = (n - 1) + n - own.astype(jnp.int32)
    pl.semaphore_wait(barrier, others)

    def left_copy(d):
        return pltpu.make_async_remote_copy(
            src_ref=left_own, dst_ref=lg_ref.at[row], send_sem=l_send.at[d], recv_sem=l_recv.at[row],
            device_id=(grp, col, lax.rem(col + d, n)), device_id_type=MESH,
        )

    def left_mask_copy(d):
        return pltpu.make_async_remote_copy(
            src_ref=mask_ref, dst_ref=ml_ref.at[row], send_sem=ml_send.at[d], recv_sem=ml_recv.at[row],
            device_id=(grp, col, lax.rem(col + d, n)), device_id_type=MESH,
        )

    def right_copy(d, g):
        piece = rg_ref.at[row, :, pl.ds(g * chunk, chunk)]
        return pltpu.make_async_remote_copy(
            src_ref=piece, dst_ref=piece, send_sem=r_send.at[d, g], recv_sem=r_recv.at[row, g],
            device_id=(grp, lax.rem(row + d, n), col), device_id_type=MESH,
        )

    def sibling_copy(j, g):
        slot = lax.rem(row + 2 * j, n)
        piece = rg_ref.at[slot, :, pl.ds(g * chunk, chunk)]
        return pltpu.make_async_remote_copy(
            src_ref=piece, dst_ref=piece, send_sem=s_send.at[j, g], recv_sem=r_recv.at[slot, g],
            device_id=(grp, sibling, col), device_id_type=MESH,
        )

    def arrived(dst, sem):
        pltpu.make_async_remote_copy(
            src_ref=dst, dst_ref=dst, send_sem=l_send.at[0], recv_sem=sem,
            device_id=(grp, sibling, col), device_id_type=MESH,
        ).wait_recv()

    def right_mask_copy(d):
        return pltpu.make_async_remote_copy(
            src_ref=mask_ref, dst_ref=mr_ref.at[row], send_sem=mr_send.at[d], recv_sem=mr_recv.at[row],
            device_id=(grp, lax.rem(row + d, n), col), device_id_type=MESH,
        )

    for d in range(1, n):
        left_mask_copy(d).start()
        right_mask_copy(d).start()

    @pl.when(jnp.logical_not(own))
    def _():
        left_mask_copy(0).start()

    for g in range(groups):
        lax.fori_loop(g * GROUP, (g + 1) * GROUP, normalize, 0, unroll=4)
        part = slice(g * chunk, (g + 1) * chunk)
        rg_ref[row, :, part] = project(norm_sj, g * chunk, chunk, wr_ref, add_right, flat_sj[:, part])
        for d in range(2, n, 2):
            right_copy(d, g).start()
        sibling_copy(0, g).start()

    def reorder(i, carry):
        at = pl.multiple_of(i * seqs, 8)
        for h in range(halves):
            norm_is[h, pl.ds(at, seqs), :] = norm_sj[h, pl.ds(i, seqs, stride=res), :]
        return carry

    lax.fori_loop(0, res, reorder, 0, unroll=4)

    left_own[...] = project(norm_is, 0, tokens, wl_ref, add_left, flat_is)
    for d in range(n - 1, 0, -1):
        left_copy(d).start()

    @pl.when(jnp.logical_not(own))
    def _():
        left_copy(0).start()

    for g in range(groups):
        for j in range(1, n // 2):
            slot = lax.rem(row + 2 * j, n)
            arrived(rg_ref.at[slot, :, pl.ds(g * chunk, chunk)], r_recv.at[slot, g])
            sibling_copy(j, g).start()

    mr_ref[row] = mask_ref[...]

    @pl.when(own)
    def _():
        lg_ref[row] = left_own[...]
        ml_ref[row] = mask_ref[...]

    width = left_own.shape[0]
    final_in[...] = wf_ref[...].astype(jnp.float32)
    for q in range(width):
        final_mid[q * width : (q + 1) * width, :] = final_in[pl.ds(q, width, stride=width), :]
    for k in range(width * width // LANES):
        part = slice(k * LANES, (k + 1) * LANES)
        wt_ref[:, part] = final_mid[part, :].T.astype(jnp.bfloat16)

    for g in range(groups):
        for d in range(2, n, 2):
            right_copy(d, g).wait_send()
        for j in range(n // 2):
            sibling_copy(j, g).wait_send()
    for d in range(1, n):
        left_mask_copy(d).wait_send()
        right_mask_copy(d).wait_send()
        left_copy(d).wait_send()

    @pl.when(jnp.logical_not(own))
    def _():
        left_mask_copy(0).wait_send()
        left_copy(0).wait_send()

    for g in range(groups):
        for j in range(n // 2):
            slot = lax.rem(sibling + 2 * j, n)
            arrived(rg_ref.at[slot, :, pl.ds(g * chunk, chunk)], r_recv.at[slot, g])
    for d in range(1, n):
        slot = lax.rem(row + d, n)
        arrived(mr_ref.at[slot], mr_recv.at[slot])
        arrived(ml_ref.at[slot], ml_recv.at[slot])
        arrived(lg_ref.at[slot], l_recv.at[slot])

    @pl.when(jnp.logical_not(own))
    def _():
        arrived(lg_ref.at[row], l_recv.at[row])
        arrived(ml_ref.at[row], ml_recv.at[row])


def pair_kernel(
    seqs, res, lg_ref, rg_ref, ml_ref, mr_ref, wt_ref, shift_ref, out_ref, stage, right, left, outer, scale, shift
):
    n, width, _ = rg_ref.shape
    block = out_ref.shape[0]
    step = pl.program_id(0)

    @pl.when(step == 0)
    def _():
        blank = jnp.zeros((width, LANES - res), jnp.float32)
        for k in range(n):
            for s in range(seqs):
                piece = rg_ref[k, :, s * res : (s + 1) * res].astype(jnp.float32)
                at = (k * seqs + s) * width
                stage[at : at + width, :] = jnp.concatenate([piece, blank], axis=1)
        for q in range(width):
            right[:, q * LANES : (q + 1) * LANES] = stage[pl.ds(q, n * seqs, stride=width), :].astype(
                jnp.bfloat16
            )
        count = lax.dot_general(
            ml_ref[...].reshape(n * seqs, LANES).astype(jnp.bfloat16),
            mr_ref[...].reshape(n * seqs, LANES).astype(jnp.bfloat16),
            (((0,), (0,)), ((), ())),
            preferred_element_type=jnp.float32,
        )
        scale[...] = 1.0 / jnp.maximum(count, 1.0)
        shift[...] = jnp.broadcast_to(column(shift_ref[...]), shift.shape)

    for i in range(block):
        left[i * width : (i + 1) * width, :] = jnp.concatenate(
            [lg_ref[k, :, i * seqs : (i + 1) * seqs] for k in range(n)], axis=1
        )

    wide = 2 * LANES

    def products(c, carry):
        at = pl.multiple_of(c * wide, wide)
        acc = jnp.dot(left[...], right[:, pl.ds(at, wide)], preferred_element_type=jnp.float32).astype(
            jnp.bfloat16
        )
        for h in range(2):
            low = pl.multiple_of((2 * c + h) * width, width)
            for i in range(block):
                outer[pl.ds(low, width), i * LANES : (i + 1) * LANES] = acc[
                    i * width : (i + 1) * width, h * LANES : (h + 1) * LANES
                ]
        return carry

    lax.fori_loop(0, width // 2, products, 0, unroll=True)

    moved = shift[...]
    for c in range(block // 2):
        acc = jnp.dot(wt_ref[...], outer[:, c * wide : (c + 1) * wide], preferred_element_type=jnp.float32)
        for h in range(2):
            i = 2 * c + h
            one = (acc[:, h * LANES : (h + 1) * LANES] + moved) * scale[pl.ds(step * block + i, 1), :]
            out_ref[i] = one.T[:res].astype(jnp.bfloat16)


def local(n, x, occupancy, gain, bias, wl, bl, wr, br, wf, bf):
    seqs, res, feat = x.shape
    width = wl.shape[1]
    pair = wf.shape[1]
    tokens = seqs * res
    whole = pl.BlockSpec(memory_space=pltpu.VMEM)
    dma = pltpu.SemaphoreType.DMA((n,))
    lg, rg, ml, mr, wt = pl.pallas_call(
        functools.partial(exchange_kernel, n),
        out_shape=(
            jax.ShapeDtypeStruct((n, width, tokens), jnp.bfloat16),
            jax.ShapeDtypeStruct((n, width, tokens), jnp.bfloat16),
            jax.ShapeDtypeStruct((n, seqs, LANES), jnp.float32),
            jax.ShapeDtypeStruct((n, seqs, LANES), jnp.float32),
            jax.ShapeDtypeStruct((pair, width * width), jnp.bfloat16),
        ),
        in_specs=[whole] * 9,
        out_specs=(whole,) * 5,
        scratch_shapes=[
            pltpu.VMEM((feat // LANES, tokens, LANES), jnp.float32),
            pltpu.VMEM((feat // LANES, tokens, LANES), jnp.float32),
            pltpu.VMEM((width, tokens), jnp.bfloat16),
            pltpu.VMEM((seqs, LANES), jnp.float32),
            pltpu.VMEM((width * width, pair), jnp.float32),
            pltpu.VMEM((width * width, pair), jnp.float32),
        ]
        + [dma] * 2
        + [pltpu.SemaphoreType.DMA((n, seqs // GROUP))] * 3
        + [dma] * 4,
        compiler_params=pltpu.CompilerParams(
            collective_id=0, has_side_effects=True, vmem_limit_bytes=VMEM_LIMIT
        ),
    )(
        x,
        gain.reshape(1, feat),
        bias.reshape(1, feat),
        wl.T,
        bl.reshape(1, width),
        wr.T,
        br.reshape(1, width),
        occupancy,
        wf,
    )
    block = 16
    depth = n * seqs

    def fixed(*shape):
        return pl.BlockSpec(shape, lambda b: (0,) * len(shape))

    return pl.pallas_call(
        functools.partial(pair_kernel, seqs, res),
        grid=(res // block,),
        out_shape=jax.ShapeDtypeStruct((res, res, pair), jnp.bfloat16),
        in_specs=[
            pl.BlockSpec((n, width, block * seqs), lambda b: (0, 0, b)),
            fixed(n, width, tokens),
            fixed(n, seqs, LANES),
            fixed(n, seqs, LANES),
            fixed(pair, width * width),
            fixed(1, pair),
        ],
        out_specs=pl.BlockSpec((block, res, pair), lambda b: (b, 0, 0)),
        scratch_shapes=[
            pltpu.VMEM((depth * width, LANES), jnp.float32),
            pltpu.VMEM((depth, width * LANES), jnp.bfloat16),
            pltpu.VMEM((block * width, depth), jnp.bfloat16),
            pltpu.VMEM((width * width, block * LANES), jnp.bfloat16),
            pltpu.VMEM((LANES, LANES), jnp.float32),
            pltpu.VMEM((pair, LANES), jnp.float32),
        ],
        compiler_params=pltpu.CompilerParams(vmem_limit_bytes=VMEM_LIMIT),
    )(lg, rg, ml, mr, wt, bf.reshape(1, pair))


def solution(mesh):
    placed = (P(("grp", "row"), "col", None), P(("grp", "row"), "col")) + (P(),) * 8
    return jax.shard_map(
        functools.partial(local, mesh.shape["row"]),
        mesh=mesh,
        in_specs=placed,
        out_specs=P(("grp", "row"), "col", None),
        check_vma=False,
    )
```

```python
import functools

import jax
import jax.numpy as jnp
from jax import lax
from jax.experimental import pallas as pl
from jax.experimental.pallas import tpu as pltpu
from jax.sharding import PartitionSpec as P

MESH = pl.DeviceIdType.MESH
LANES = 128
VMEM_LIMIT = 56 * 1024 * 1024


def column(line):
    size = line.shape[1]
    down = lax.broadcasted_iota(jnp.int32, (size, size), 0)
    across = lax.broadcasted_iota(jnp.int32, (size, size), 1)
    return jnp.sum(jnp.where(down == across, line, 0.0), axis=1, keepdims=True)


def exchange_kernel(
    n,
    x_ref,
    gain_ref,
    bias_ref,
    wl_ref,
    bl_ref,
    wr_ref,
    br_ref,
    occ_ref,
    wf_ref,
    lg_ref,
    rg_ref,
    ml_ref,
    mr_ref,
    wt_ref,
    norm_sj,
    norm_is,
    left_own,
    mask_ref,
    final_in,
    final_mid,
    l_send,
    l_recv,
    r_send,
    r_recv,
    ml_send,
    ml_recv,
    mr_send,
    mr_recv,
):
    seqs, res, feat = x_ref.shape
    halves = feat // LANES
    tokens = seqs * res
    grp = lax.axis_index("grp")
    row = lax.axis_index("row")
    col = lax.axis_index("col")
    own = row == col

    barrier = pltpu.get_barrier_semaphore()
    for d in range(1, n):
        pl.semaphore_signal(barrier, inc=1, device_id=(grp, lax.rem(row + d, n), col), device_id_type=MESH)
        pl.semaphore_signal(barrier, inc=1, device_id=(grp, lax.rem(row + d, n), row), device_id_type=MESH)

    @pl.when(jnp.logical_not(own))
    def _():
        pl.semaphore_signal(barrier, inc=1, device_id=(grp, row, row), device_id_type=MESH)

    gain = gain_ref[...]
    bias = bias_ref[...]
    occ = occ_ref[...].astype(jnp.float32)
    mask_ref[...] = jnp.concatenate([occ, jnp.zeros((seqs, LANES - res), jnp.float32)], axis=1)
    flat_sj = jnp.concatenate([occ[s : s + 1] for s in range(seqs)], axis=1)
    turned = mask_ref[...].T[:res]
    flat_is = jnp.concatenate([turned[i : i + 1] for i in range(res)], axis=1)

    def normalize(s, carry):
        e = x_ref[s].astype(jnp.float32)
        center = e - jnp.mean(e, axis=-1, keepdims=True)
        spread = jnp.mean(center * center, axis=-1, keepdims=True)
        v = center * lax.rsqrt(spread + 1e-05) * gain + bias
        at = pl.multiple_of(s * res, 8)
        for h in range(halves):
            norm_sj[h, pl.ds(at, res), :] = v[:, h * LANES : (h + 1) * LANES]
        return carry

    lax.fori_loop(0, seqs, normalize, 0, unroll=4)

    def reorder(i, carry):
        at = pl.multiple_of(i * seqs, 8)
        for h in range(halves):
            norm_is[h, pl.ds(at, seqs), :] = norm_sj[h, pl.ds(i, seqs, stride=res), :]
        return carry

    lax.fori_loop(0, res, reorder, 0, unroll=4)

    def project(src, w_ref, b_ref, flat):
        total = column(b_ref[...])
        acc = None
        for h in range(halves):
            part = lax.dot_general(
                w_ref[:, h * LANES : (h + 1) * LANES],
                src[h].astype(jnp.bfloat16),
                (((1,), (1,)), ((), ())),
                preferred_element_type=jnp.float32,
            )
            acc = part if acc is None else acc + part
        return ((acc + total) * flat).astype(jnp.bfloat16)

    left_own[...] = project(norm_is, wl_ref, bl_ref, flat_is)

    others = (n - 1) + n - own.astype(jnp.int32)
    pl.semaphore_wait(barrier, others)

    def left_copies(d):
        target = (grp, col, lax.rem(col + d, n))
        return (
            pltpu.make_async_remote_copy(
                src_ref=left_own, dst_ref=lg_ref.at[row], send_sem=l_send.at[d], recv_sem=l_recv.at[row],
                device_id=target, device_id_type=MESH,
            ),
            pltpu.make_async_remote_copy(
                src_ref=mask_ref, dst_ref=ml_ref.at[row], send_sem=ml_send.at[d], recv_sem=ml_recv.at[row],
                device_id=target, device_id_type=MESH,
            ),
        )

    def right_copies(d):
        target = (grp, lax.rem(row + d, n), col)
        return (
            pltpu.make_async_remote_copy(
                src_ref=rg_ref.at[row], dst_ref=rg_ref.at[row], send_sem=r_send.at[d], recv_sem=r_recv.at[row],
                device_id=target, device_id_type=MESH,
            ),
            pltpu.make_async_remote_copy(
                src_ref=mask_ref, dst_ref=mr_ref.at[row], send_sem=mr_send.at[d], recv_sem=mr_recv.at[row],
                device_id=target, device_id_type=MESH,
            ),
        )

    for d in range(1, n):
        for copy in left_copies(d):
            copy.start()

    @pl.when(jnp.logical_not(own))
    def _():
        for copy in left_copies(0):
            copy.start()

    rg_ref[row] = project(norm_sj, wr_ref, br_ref, flat_sj)
    for d in range(1, n):
        for copy in right_copies(d):
            copy.start()

    mr_ref[row] = mask_ref[...]

    @pl.when(own)
    def _():
        lg_ref[row] = left_own[...]
        ml_ref[row] = mask_ref[...]

    width = left_own.shape[0]
    final_in[...] = wf_ref[...].astype(jnp.float32)
    for q in range(width):
        final_mid[q * width : (q + 1) * width, :] = final_in[pl.ds(q, width, stride=width), :]
    for k in range(width * width // LANES):
        part = slice(k * LANES, (k + 1) * LANES)
        wt_ref[:, part] = final_mid[part, :].T.astype(jnp.bfloat16)

    for d in range(1, n):
        for copy in left_copies(d) + right_copies(d):
            copy.wait_send()

    @pl.when(jnp.logical_not(own))
    def _():
        for copy in left_copies(0):
            copy.wait_send()

    def arrived(dst, slot, sem):
        pltpu.make_async_remote_copy(
            src_ref=dst.at[slot], dst_ref=dst.at[slot], send_sem=l_send.at[0], recv_sem=sem.at[slot],
            device_id=(grp, lax.rem(row + 1, n), col), device_id_type=MESH,
        ).wait_recv()

    for d in range(1, n):
        slot = lax.rem(row + d, n)
        arrived(rg_ref, slot, r_recv)
        arrived(mr_ref, slot, mr_recv)
        arrived(lg_ref, slot, l_recv)
        arrived(ml_ref, slot, ml_recv)

    @pl.when(jnp.logical_not(own))
    def _():
        arrived(lg_ref, row, l_recv)
        arrived(ml_ref, row, ml_recv)


def pair_kernel(
    seqs, res, lg_ref, rg_ref, ml_ref, mr_ref, wt_ref, shift_ref, out_ref, stage, right, left, outer, scale, shift
):
    n, width, _ = rg_ref.shape
    block = out_ref.shape[0]
    step = pl.program_id(0)

    @pl.when(step == 0)
    def _():
        blank = jnp.zeros((width, LANES - res), jnp.float32)
        for k in range(n):
            for s in range(seqs):
                piece = rg_ref[k, :, s * res : (s + 1) * res].astype(jnp.float32)
                at = (k * seqs + s) * width
                stage[at : at + width, :] = jnp.concatenate([piece, blank], axis=1)
        for q in range(width):
            right[:, q * LANES : (q + 1) * LANES] = stage[pl.ds(q, n * seqs, stride=width), :].astype(
                jnp.bfloat16
            )
        count = lax.dot_general(
            ml_ref[...].reshape(n * seqs, LANES).astype(jnp.bfloat16),
            mr_ref[...].reshape(n * seqs, LANES).astype(jnp.bfloat16),
            (((0,), (0,)), ((), ())),
            preferred_element_type=jnp.float32,
        )
        scale[...] = 1.0 / jnp.maximum(count, 1.0)
        shift[...] = jnp.broadcast_to(column(shift_ref[...]), shift.shape)

    for i in range(block):
        left[i * width : (i + 1) * width, :] = jnp.concatenate(
            [lg_ref[k, :, i * seqs : (i + 1) * seqs] for k in range(n)], axis=1
        )

    wide = 2 * LANES

    def products(c, carry):
        at = pl.multiple_of(c * wide, wide)
        acc = jnp.dot(left[...], right[:, pl.ds(at, wide)], preferred_element_type=jnp.float32).astype(
            jnp.bfloat16
        )
        for h in range(2):
            low = pl.multiple_of((2 * c + h) * width, width)
            for i in range(block):
                outer[pl.ds(low, width), i * LANES : (i + 1) * LANES] = acc[
                    i * width : (i + 1) * width, h * LANES : (h + 1) * LANES
                ]
        return carry

    lax.fori_loop(0, width // 2, products, 0, unroll=True)

    moved = shift[...]
    for c in range(block // 2):
        acc = jnp.dot(wt_ref[...], outer[:, c * wide : (c + 1) * wide], preferred_element_type=jnp.float32)
        for h in range(2):
            i = 2 * c + h
            one = (acc[:, h * LANES : (h + 1) * LANES] + moved) * scale[pl.ds(step * block + i, 1), :]
            out_ref[i] = one.T[:res].astype(jnp.bfloat16)


def local(n, x, occupancy, gain, bias, wl, bl, wr, br, wf, bf):
    seqs, res, feat = x.shape
    width = wl.shape[1]
    pair = wf.shape[1]
    tokens = seqs * res
    whole = pl.BlockSpec(memory_space=pltpu.VMEM)
    dma = pltpu.SemaphoreType.DMA((n,))
    lg, rg, ml, mr, wt = pl.pallas_call(
        functools.partial(exchange_kernel, n),
        out_shape=(
            jax.ShapeDtypeStruct((n, width, tokens), jnp.bfloat16),
            jax.ShapeDtypeStruct((n, width, tokens), jnp.bfloat16),
            jax.ShapeDtypeStruct((n, seqs, LANES), jnp.float32),
            jax.ShapeDtypeStruct((n, seqs, LANES), jnp.float32),
            jax.ShapeDtypeStruct((pair, width * width), jnp.bfloat16),
        ),
        in_specs=[whole] * 9,
        out_specs=(whole,) * 5,
        scratch_shapes=[
            pltpu.VMEM((feat // LANES, tokens, LANES), jnp.float32),
            pltpu.VMEM((feat // LANES, tokens, LANES), jnp.float32),
            pltpu.VMEM((width, tokens), jnp.bfloat16),
            pltpu.VMEM((seqs, LANES), jnp.float32),
            pltpu.VMEM((width * width, pair), jnp.float32),
            pltpu.VMEM((width * width, pair), jnp.float32),
        ]
        + [dma] * 8,
        compiler_params=pltpu.CompilerParams(
            collective_id=0, has_side_effects=True, vmem_limit_bytes=VMEM_LIMIT
        ),
    )(
        x,
        gain.reshape(1, feat),
        bias.reshape(1, feat),
        wl.T,
        bl.reshape(1, width),
        wr.T,
        br.reshape(1, width),
        occupancy,
        wf,
    )
    block = 16
    depth = n * seqs

    def fixed(*shape):
        return pl.BlockSpec(shape, lambda b: (0,) * len(shape))

    return pl.pallas_call(
        functools.partial(pair_kernel, seqs, res),
        grid=(res // block,),
        out_shape=jax.ShapeDtypeStruct((res, res, pair), jnp.bfloat16),
        in_specs=[
            pl.BlockSpec((n, width, block * seqs), lambda b: (0, 0, b)),
            fixed(n, width, tokens),
            fixed(n, seqs, LANES),
            fixed(n, seqs, LANES),
            fixed(pair, width * width),
            fixed(1, pair),
        ],
        out_specs=pl.BlockSpec((block, res, pair), lambda b: (b, 0, 0)),
        scratch_shapes=[
            pltpu.VMEM((depth * width, LANES), jnp.float32),
            pltpu.VMEM((depth, width * LANES), jnp.bfloat16),
            pltpu.VMEM((block * width, depth), jnp.bfloat16),
            pltpu.VMEM((width * width, block * LANES), jnp.bfloat16),
            pltpu.VMEM((LANES, LANES), jnp.float32),
            pltpu.VMEM((pair, LANES), jnp.float32),
        ],
        compiler_params=pltpu.CompilerParams(vmem_limit_bytes=VMEM_LIMIT),
    )(lg, rg, ml, mr, wt, bf.reshape(1, pair))


def solution(mesh):
    placed = (P(("grp", "row"), "col", None), P(("grp", "row"), "col")) + (P(),) * 8
    return jax.shard_map(
        functools.partial(local, mesh.shape["row"]),
        mesh=mesh,
        in_specs=placed,
        out_specs=P(("grp", "row"), "col", None),
        check_vma=False,
    )
```
